32 devices in a mesh: cells: 8 (over z, x), genes: 4 (over y, core).
Axes of the slice: x: 2, y: 2, z: 4, core: 2. Of those that a mesh axis runs over, the one named last changes fastest.
Arguments:
- counts: int32 [2000, 49152], P('genes', 'cells'), may hold values from 0 to 21, as said below
- start_basis: float32 [2000, 64], P('genes'), may hold values from -6 to 6
Outputs:
- embeddings: float32 [49152, 64], P(('cells', 'genes'))
The draws below stay inside these ranges and needn't reach their ends.
Inputs may be any that keep to these rules, and one draw needn't show every extreme that they name: `counts`: every cell has at least one nonzero count.
All inputs are finite; a program needn't handle non-finite values.
Results may differ from the reference program's by a relative error of at most 0.00015.
Values sent between devices are 32-bit elements; how exact they have to be, the bound alone decides.
A program may use at most 128 MiB of HBM per device.

```python
import math
import jax
import jax.numpy as jnp
from jax import lax

G = 2000
R = 64
ITERS = 2
C_DEV = 6144
CELLS = 49152


def draw_counts(key, part):
    key_rate, key_depth, key_present, key_value, key_forced = jax.random.split(key, 5)
    gene_ids = jnp.arange(G, dtype=jnp.int32)
    cell_ids = jnp.arange(CELLS, dtype=jnp.int32)
    set_cells = CELLS // 2
    position = cell_ids % set_cells
    rate_code = jax.random.randint(key_rate, (G,), 2, 9, dtype=jnp.int32) + 4 * gene_ids // G
    threshold = jnp.left_shift(jnp.ones((G,), jnp.int32), rate_code)
    depth_top = 3 + 8 * position // set_cells
    depth = jax.random.randint(key_depth, (CELLS,), 1, depth_top + 1, dtype=jnp.int32)
    uniform_draw = jax.random.randint(key_present, (G, CELLS), 0, 4096, dtype=jnp.int32)
    values = 1 + jax.random.randint(key_value, (G, CELLS), 0, 2 * depth[None, :], dtype=jnp.int32)
    present = uniform_draw < threshold[:, None] * depth[None, :]
    forced = jax.random.randint(key_forced, (CELLS,), 0, G, dtype=jnp.int32)
    extra = (gene_ids[:, None] == forced[None, :]).astype(jnp.int32)
    return jnp.where(present, values, 0) + extra


def levels(key, dims, cuts, low, top_value):
    def one(dim, parts):
        draws = jax.random.uniform(jax.random.fold_in(jax.random.fold_in(key, 6), dim), (parts,), jnp.float32, low / len(cuts), top_value / len(cuts))
        return jnp.repeat(jnp.exp(draws), dims[dim] // parts).reshape((-1,) + (1,) * (len(dims) - dim - 1))

    factor_of = one(*cuts[0])
    for cut in cuts[1:]:
        factor_of = factor_of * one(*cut)
    return factor_of


def noise(stream_key, dims, scale, most, cuts=(), kind=jnp.bfloat16):
    gain = levels(stream_key, dims, cuts, -0.22, 0.18) if cuts else 1.0
    array = jax.random.normal(stream_key, dims, jnp.float32) * scale * gain
    return jnp.minimum(jnp.maximum(array, -most), most).astype(kind)


def setup_inputs(seed: int = 0) -> dict:
    splits = jax.random.split(jax.random.key(seed), 3)
    return {
        "counts": draw_counts(jax.random.fold_in(splits[2], 71), 0),
        "start_basis": noise(splits[1], (G, R), 1.0, 6.0, ((0, 4),), jnp.float32),
    }


epsilon = 1e-05
clip_top = 10.0
highest = lax.Precision.HIGHEST

def orthonormal(matrix):
    gram_set = jnp.dot(matrix.T, matrix, precision=highest)
    factor = jnp.linalg.cholesky(gram_set)
    return jax.scipy.linalg.solve_triangular(factor, matrix.T, lower=True).T

def reference(counts, start_basis):
    gene_count, total_cells = counts.shape
    rank_cols = start_basis.shape[1]
    set_cells = total_cells // 2
    block_cols = C_DEV
    per_set = set_cells // block_cols

    def raw_block(index):
        return lax.dynamic_slice_in_dim(counts, index * block_cols, block_cols, 1).astype(jnp.float32)
    totals = lax.map(lambda index: lax.optimization_barrier(jnp.sum(raw_block(index), axis=0)), jnp.arange(2 * per_set, dtype=jnp.int32))

    def log_block(index):
        return jnp.log1p(10000.0 * raw_block(index) / totals[index][None, :])

    def set_sum(dataset, fn, init):

        def sweep(carried, inner):
            return (carried + fn(dataset * per_set + inner, inner), None)
        return lax.scan(sweep, init, jnp.arange(per_set, dtype=jnp.int32))[0]
    zero_genes = jnp.zeros((gene_count,), jnp.float32)
    centers = []
    deviations = []
    for dataset in range(2):
        center = set_sum(dataset, lambda index, inner: lax.optimization_barrier(jnp.sum(log_block(index), axis=1)), zero_genes) / set_cells
        spread = set_sum(dataset, lambda index, inner: lax.optimization_barrier(jnp.sum(jnp.square(log_block(index) - center[:, None]), axis=1)), zero_genes) / set_cells
        centers.append(center)
        deviations.append(jnp.sqrt(spread + epsilon))

    def scaled_block(dataset, index):
        return jnp.minimum((log_block(index) - centers[dataset][:, None]) / deviations[dataset][:, None], clip_top)

    def project(dataset, weight):

        def one_block(inner):
            return lax.dot_general(scaled_block(dataset, dataset * per_set + inner), weight, (((0,), (0,)), ((), ())), precision=highest)
        pieces = lax.map(one_block, jnp.arange(per_set, dtype=jnp.int32))
        return pieces.reshape(set_cells, rank_cols)

    def product(dataset, basis):

        def one_block(index, inner):
            rows_here = lax.dynamic_slice_in_dim(basis, inner * block_cols, block_cols, 0)
            return jnp.dot(scaled_block(dataset, index), rows_here, precision=highest)
        return set_sum(dataset, one_block, jnp.zeros((gene_count, rank_cols), jnp.float32))
    bases = [orthonormal(project(0, start_basis)), orthonormal(project(1, start_basis))]
    for sweep_index in range(ITERS):
        products = [product(0, bases[0]), product(1, bases[1])]
        bases = [orthonormal(project(0, products[1])), orthonormal(project(1, products[0]))]
    return jnp.concatenate(bases, axis=0) * math.sqrt(set_cells)
```

```python
import functools
import math

import jax
import jax.numpy as jnp
from jax import lax
from jax.experimental import pallas as pl
from jax.experimental.pallas import tpu as pltpu
from jax.sharding import PartitionSpec as P

ITERS = 2
epsilon = 1e-05
clip_top = 10.0
highest = lax.Precision.HIGHEST
f32 = jnp.float32
bf16 = jnp.bfloat16
LANES = 128
NT = (((1,), (1,)), ((), ()))


def split_two(value):
    high = value.astype(bf16)
    return high, (value - high.astype(f32)).astype(bf16)


def split_three(value):
    high = value.astype(bf16)
    rest = value - high.astype(f32)
    middle, low = split_two(rest)
    return high, middle, low


def inverse_factor(gram_folded):
    half_rows = gram_folded.shape[0]
    rank = 2 * half_rows
    lane = lax.broadcasted_iota(jnp.int32, (rank, 2 * rank), 1)
    row = lax.broadcasted_iota(jnp.int32, (rank, 2 * rank), 0)
    row_column = lax.broadcasted_iota(jnp.int32, (rank, 1), 0)
    gram = jnp.concatenate([gram_folded, pltpu.roll(gram_folded, rank, 1)], axis=0)
    both = jnp.where(lane < rank, gram, jnp.where(lane == row + rank, 1.0, 0.0))

    def step(k, both):
        pivot_row = jnp.sum(jnp.where(row == k, both, 0.0), axis=0, keepdims=True)
        column = jnp.sum(jnp.where(lane == k, both, 0.0), axis=1, keepdims=True)
        pivot = jnp.sum(jnp.where(row_column == k, column, 0.0), axis=0, keepdims=True)
        factor = jnp.where(row_column > k, column / pivot, 0.0)
        return both - factor * pivot_row

    both = lax.fori_loop(0, rank, step, both)
    diagonal = jnp.sum(jnp.where(lane == row, both, 0.0), axis=1, keepdims=True)
    return both[:, rank:] * lax.rsqrt(diagonal)


def kernel(
    cfg, counts_ref, basis_ref, out_ref,
    cnt, logs, xhi, xlo, tot, acc, center_ref, scale_ref, stat, wsplit,
    send_a, recv_a, send_b, recv_b, own_p, recv_p, product, gram_acc, inverse,
    shares, quarter_out, quarter_in, whole, gram_g, gram_c,
    load_sem, tot_sem, stat_sem, a_sem, b_send, b_recv, c_sem, rs_sem, x_sem, ag_sem, gg_sem, gc_sem,
):
    genes_dev, cells_dev, rank, groups, cell_devs, chunk, share_rows = cfg
    half_devs = cell_devs // 2
    set_cells = cells_dev * half_devs
    quarter = cells_dev // groups
    per_quarter = quarter // chunk
    steps = 2 * per_quarter
    gene = lax.axis_index("genes")
    cell = lax.axis_index("cells")
    y, core = gene // 2, gene % 2
    core_mate = {"genes": y * 2 + 1 - core}
    y_mate = {"genes": (1 - y) * 2 + core}
    dataset = cell // half_devs
    place = cell % half_devs
    cross = {"cells": (1 - dataset) * half_devs + place}

    def gene_peer(i):
        return {"genes": (gene + i) % groups}

    def set_place(i):
        return (place + i) % half_devs

    def set_peer(i):
        return {"cells": dataset * half_devs + set_place(i)}

    def remote(src, dst, send, recv, device):
        return pltpu.make_async_remote_copy(
            src_ref=src, dst_ref=dst, send_sem=send, recv_sem=recv,
            device_id=device, device_id_type=pl.DeviceIdType.MESH,
        )

    load_cols = cells_dev // 6 if cells_dev % (6 * LANES) == 0 else cells_dev
    loads = []
    for i in range(cells_dev // load_cols):
        cols = pl.ds(i * load_cols, load_cols)
        copy = pltpu.make_async_copy(counts_ref.at[:, cols], cnt.at[:, cols], load_sem.at[i])
        copy.start()
        loads.append(copy)

    barrier = pltpu.get_barrier_semaphore()
    mates = [gene_peer(i) for i in range(1, groups)]
    mates += [set_peer(i) for i in range(1, half_devs)] + [cross]
    for mate in mates:
        pl.semaphore_signal(barrier, inc=1, device_id=mate, device_id_type=pl.DeviceIdType.MESH)

    acc[...] = jnp.zeros_like(acc)
    stat[0] = jnp.zeros(stat.shape[1:], f32)
    for i, piece in enumerate(split_three(basis_ref[...])):
        wsplit[i * rank : (i + 1) * rank, :] = piece

    for i, copy in enumerate(loads):
        copy.wait()

        def add_genes(j, carry, base=i * load_cols):
            cols = pl.ds(pl.multiple_of(base + j * LANES, LANES), LANES)
            tot[0, :, cols] = jnp.sum(cnt[:, cols], axis=0, keepdims=True).astype(f32)
            return carry

        lax.fori_loop(0, load_cols // LANES, add_genes, 0)
    pl.semaphore_wait(barrier, len(mates))
    copies = [
        remote(tot.at[0], tot.at[i], tot_sem.at[0, i], tot_sem.at[1, i], gene_peer(i))
        for i in range(1, groups)
    ]
    for copy in copies:
        copy.start()
    for copy in copies:
        copy.wait()

    def to_logs(j, carry):
        cols = pl.ds(pl.multiple_of(j * LANES, LANES), LANES)
        total = tot[0, :, cols]
        for i in range(1, groups):
            total = total + tot[i, :, cols]
        value = jnp.log(1.0 + cnt[:, cols].astype(f32) * (10000.0 / total))
        logs[:, cols] = value
        acc[0:genes_dev, :] += value
        return carry

    lax.fori_loop(0, cells_dev // LANES, to_logs, 0)
    stat[0, 0:1, :] = jnp.sum(acc[...].T, axis=0, keepdims=True)
    center_ref[...] = jnp.broadcast_to(
        jnp.sum(acc[...], axis=1, keepdims=True) * (1.0 / cells_dev), center_ref.shape
    )
    acc[...] = jnp.zeros_like(acc)

    def add_squares(j, carry):
        cols = pl.ds(pl.multiple_of(j * LANES, LANES), LANES)
        centered = logs[:, cols] - center_ref[0:genes_dev, :]
        acc[0:genes_dev, :] += centered * centered
        return carry

    lax.fori_loop(0, cells_dev // LANES, add_squares, 0)
    stat[0, 1:2, :] = jnp.sum(acc[...].T, axis=0, keepdims=True)
    copies = [
        remote(stat.at[0], stat.at[i], stat_sem.at[0, i], stat_sem.at[1, i], set_peer(i))
        for i in range(1, half_devs)
    ]
    for copy in copies:
        copy.start()
    for copy in copies:
        copy.wait()
    gene_sum = stat[0, 0:1, :]
    for i in range(1, half_devs):
        gene_sum = gene_sum + stat[i, 0:1, :]
    center = gene_sum * (1.0 / set_cells)
    squares = jnp.zeros_like(center)
    for i in range(half_devs):
        shift = stat[i, 0:1, :] * (1.0 / cells_dev) - center
        squares = squares + (stat[i, 1:2, :] + cells_dev * (shift * shift))
    scale = 1.0 / jnp.sqrt(squares * (1.0 / set_cells) + epsilon)
    wide = (LANES, center.shape[1])
    center_ref[...] = jnp.broadcast_to(center, wide).T
    scale_ref[...] = jnp.broadcast_to(scale, wide).T

    def offset(k, half):
        return pl.multiple_of(
            (k // per_quarter) * (2 * quarter) + half * quarter + (k % per_quarter) * chunk, LANES
        )

    def scale_chunk(start):
        def part(j, carry):
            cols = pl.ds(pl.multiple_of(start + j * LANES, LANES), LANES)
            value = (logs[:, cols] - center_ref[0:genes_dev, :]) * scale_ref[0:genes_dev, :]
            high, low = split_two(jnp.minimum(value, clip_top))
            xhi[:, cols] = high
            xlo[:, cols] = low
            return carry

        lax.fori_loop(0, chunk // LANES, part, 0)

    def project(start):
        cols = pl.ds(start, chunk)
        top = jnp.dot(wsplit[...], xhi[:, cols], preferred_element_type=f32)
        rest = jnp.dot(wsplit[0 : 2 * rank, :], xlo[:, cols], preferred_element_type=f32)
        small = top[2 * rank :] + rest[rank:]
        return top[0:rank] + (top[rank : 2 * rank] + rest[0:rank] + small)

    def copy_a(k):
        return remote(send_a.at[k], recv_a.at[k], a_sem.at[0, k], a_sem.at[1, k], core_mate)

    def copy_c(k):
        return remote(own_p.at[k], recv_p.at[k], c_sem.at[0, k], c_sem.at[1, k], core_mate)

    def copy_b(stage, k, slot):
        return remote(
            send_b.at[k], recv_b.at[stage, slot], b_send.at[slot], b_recv.at[stage, slot], y_mate
        )

    def chip_sum(k, first):
        other = offset(k, 1 - core)
        if first:
            scale_chunk(other)
        send_a[k] = project(other)
        copy_a(k).start()
        mine = offset(k, core)
        if first:
            scale_chunk(mine)
        value = project(mine)
        copy_a(k).wait_recv()
        send_b[k] = value + recv_a[k]

    def add_gram(pieces):
        gram_acc[...] += lax.dot_general(pieces, pieces, NT, preferred_element_type=f32)

    def pieces_of(value):
        return jnp.concatenate(split_two(value), axis=0)

    def add_product(value, start):
        cols = pl.ds(start, chunk)
        pieces = pieces_of(value)
        product[0:genes_dev, :] += lax.dot_general(
            xhi[:, cols], pieces, NT, preferred_element_type=f32
        ) + lax.dot_general(xlo[:, cols], pieces, NT, preferred_element_type=f32)
        add_gram(pieces)

    lane_g = lax.broadcasted_iota(jnp.int32, (rank // 2, 2 * rank), 1)

    def folded_gram():
        gram = gram_acc[0:rank, :] + gram_acc[rank:, :]
        gram = gram + pltpu.roll(gram, rank, 1)
        return jnp.where(lane_g < rank, gram[0 : rank // 2], gram[rank // 2 :])

    fold = product.shape[0] // 2
    last = ITERS
    for stage in range(ITERS):
        def first_loop(k, carry, stage=stage):
            chip_sum(k, stage == 0)
            copy_b(stage, k, k).start()
            return carry

        lax.fori_loop(0, steps, first_loop, 0)
        product[...] = jnp.zeros_like(product)
        gram_acc[...] = jnp.zeros_like(gram_acc)
        if stage > 0:
            inverse[...] = inverse_factor(whole[stage - 1, fold : fold + rank // 2, :])

        def second_loop(k, carry, stage=stage):
            copy_b(stage, k, k).wait()
            value = send_b[k] + recv_b[stage, k]
            if stage > 0:
                value = jnp.dot(inverse[...], value, precision=highest, preferred_element_type=f32)
            own_p[k] = value
            copy_c(k).start()
            add_product(value, offset(k, core))
            copy_a(k).wait_send()
            copy_c(k).wait()
            add_product(recv_p[k], offset(k, 1 - core))
            return carry

        lax.fori_loop(0, steps, second_loop, 0)

        lane = lax.broadcasted_iota(jnp.int32, (fold, 2 * rank), 1)
        summed = product[...] + pltpu.roll(product[...], rank, 1)
        local = whole.at[ITERS + stage]
        local[0:fold, :] = jnp.where(lane < rank, summed[0:fold], summed[fold:])
        local[fold : fold + rank // 2, :] = folded_gram()
        if local.shape[0] > fold + rank // 2:
            rest = local.shape[0] - fold - rank // 2
            local[fold + rank // 2 :, :] = jnp.zeros((rest, 2 * rank), f32)

        def rows_of(index):
            return pl.ds(pl.multiple_of(index * share_rows, 8), share_rows)

        copies = [
            remote(
                local.at[rows_of(set_place(i))], shares.at[stage, i],
                rs_sem.at[0, stage, i], rs_sem.at[1, stage, i], set_peer(i),
            )
            for i in range(1, half_devs)
        ]
        for copy in copies:
            copy.start()
        for copy in copies:
            copy.wait()
        value = local[rows_of(place), :]
        for i in range(1, half_devs):
            value = value + shares[stage, i]
        quarter_out[stage] = value
        copy = remote(
            quarter_out.at[stage], quarter_in.at[stage], x_sem.at[0, stage], x_sem.at[1, stage], cross
        )
        copy.start()
        copy.wait()
        mine = rows_of(place)
        copies = [
            remote(
                quarter_in.at[stage], whole.at[stage, mine],
                ag_sem.at[0, stage, i], ag_sem.at[1, stage, i], set_peer(i),
            )
            for i in range(1, half_devs)
        ]
        for copy in copies:
            copy.start()
        whole[stage, mine, :] = quarter_in[stage]
        for copy in copies:
            copy.wait()
        turned = whole[stage, 0:fold, :].T
        for part, rows in ((0, turned[0:rank]), (1, turned[rank:])):
            width = min(fold, genes_dev - part * fold)
            for i, piece in enumerate(split_three(rows[:, 0:width])):
                wsplit[i * rank : (i + 1) * rank, part * fold : part * fold + width] = piece

    def send_loop(j, carry):
        k = (1 - y) * per_quarter + j
        chip_sum(k, False)
        copy_b(last, k, j).start()
        return carry

    lax.fori_loop(0, per_quarter, send_loop, 0)

    def keep_loop(j, carry):
        chip_sum(y * per_quarter + j, False)
        return carry

    lax.fori_loop(0, per_quarter, keep_loop, 0)
    gram_acc[...] = jnp.zeros_like(gram_acc)
    inverse[...] = inverse_factor(whole[ITERS - 1, fold : fold + rank // 2, :])

    def last_loop(j, carry):
        copy_b(last, y * per_quarter + j, j).wait()
        value = send_b[y * per_quarter + j] + recv_b[last, j]
        value = jnp.dot(inverse[...], value, precision=highest, preferred_element_type=f32)
        own_p[j] = value
        add_gram(pieces_of(value))
        copy_a(j).wait_send()
        copy_a(j + per_quarter).wait_send()
        return carry

    lax.fori_loop(0, per_quarter, last_loop, 0)
    gram_g[0] = folded_gram()
    copies = [
        remote(gram_g.at[0], gram_g.at[i], gg_sem.at[0, i], gg_sem.at[1, i], gene_peer(i))
        for i in range(1, groups)
    ]
    for copy in copies:
        copy.start()
    for copy in copies:
        copy.wait()
    value = gram_g[0]
    for i in range(1, groups):
        value = value + gram_g[i]
    gram_c[0] = value
    copies = [
        remote(gram_c.at[0], gram_c.at[i], gc_sem.at[0, i], gc_sem.at[1, i], set_peer(i))
        for i in range(1, half_devs)
    ]
    for copy in copies:
        copy.start()
    for copy in copies:
        copy.wait()
    for i in range(1, half_devs):
        value = value + gram_c[i]
    inverse[...] = inverse_factor(value) * math.sqrt(set_cells)
    for j in range(per_quarter):
        out_ref[:, j * chunk : (j + 1) * chunk] = jnp.dot(
            inverse[...], own_p[j], precision=highest, preferred_element_type=f32
        )


def shards(counts, start_basis):
    genes_dev, cells_dev = counts.shape
    rank = start_basis.shape[1]
    groups = lax.axis_size("genes")
    cell_devs = lax.axis_size("cells")
    assert groups == 4 and rank == 64
    half_devs = cell_devs // 2
    quarter = cells_dev // groups
    chunk = max(c for c in range(LANES, 512 + 1, LANES) if quarter % c == 0)
    steps = 2 * quarter // chunk
    padded = -(-genes_dev // 256) * 256
    rows = padded // 2 + rank // 2
    share_rows = -(-rows // (8 * half_devs)) * 8
    block = (rank, chunk)
    dma = pltpu.SemaphoreType.DMA
    scratch = [
        pltpu.VMEM((genes_dev, cells_dev), jnp.int32),
        pltpu.VMEM((genes_dev, cells_dev), f32),
        pltpu.VMEM((genes_dev, cells_dev), bf16),
        pltpu.VMEM((genes_dev, cells_dev), bf16),
        pltpu.VMEM((groups, 1, cells_dev), f32),
        pltpu.VMEM((padded, LANES), f32),
        pltpu.VMEM((padded, LANES), f32),
        pltpu.VMEM((padded, LANES), f32),
        pltpu.VMEM((half_devs, 8, padded), f32),
        pltpu.VMEM((3 * rank, genes_dev), bf16),
        pltpu.VMEM((steps,) + block, f32),
        pltpu.VMEM((steps,) + block, f32),
        pltpu.VMEM((steps,) + block, f32),
        pltpu.VMEM((ITERS + 1, steps) + block, f32),
        pltpu.VMEM((steps,) + block, f32),
        pltpu.VMEM((steps,) + block, f32),
        pltpu.VMEM((padded, 2 * rank), f32),
        pltpu.VMEM((2 * rank, 2 * rank), f32),
        pltpu.VMEM((rank, rank), f32),
        pltpu.VMEM((ITERS, half_devs, share_rows, 2 * rank), f32),
        pltpu.VMEM((ITERS, share_rows, 2 * rank), f32),
        pltpu.VMEM((ITERS, share_rows, 2 * rank), f32),
        pltpu.VMEM((2 * ITERS, share_rows * half_devs, 2 * rank), f32),
        pltpu.VMEM((groups, rank // 2, 2 * rank), f32),
        pltpu.VMEM((half_devs, rank // 2, 2 * rank), f32),
        dma((6,)),
        dma((2, groups)),
        dma((2, half_devs)),
        dma((2, steps)),
        dma((steps,)),
        dma((ITERS + 1, steps)),
        dma((2, steps)),
        dma((2, ITERS, half_devs)),
        dma((2, ITERS)),
        dma((2, ITERS, half_devs)),
        dma((2, groups)),
        dma((2, half_devs)),
    ]
    cfg = (genes_dev, cells_dev, rank, groups, cell_devs, chunk, share_rows)
    flops = 2 * 5 * 4 * genes_dev * cells_dev * rank
    turned = pl.pallas_call(
        functools.partial(kernel, cfg),
        out_shape=jax.ShapeDtypeStruct((rank, quarter), f32),
        in_specs=[pl.BlockSpec(memory_space=pl.ANY), pl.BlockSpec(memory_space=pltpu.VMEM)],
        out_specs=pl.BlockSpec(memory_space=pltpu.VMEM),
        scratch_shapes=scratch,
        compiler_params=pltpu.CompilerParams(
            collective_id=0, has_side_effects=True, vmem_limit_bytes=60 * 2**20
        ),
        cost_estimate=pl.CostEstimate(
            flops=flops, bytes_accessed=4 * genes_dev * cells_dev,
            transcendentals=genes_dev * cells_dev,
        ),
    )(counts, start_basis.T)
    return turned.T


def solution(mesh):
    placed = (P("genes", "cells"), P("genes", None))
    return jax.shard_map(
        shards, mesh=mesh, in_specs=placed, out_specs=P(("cells", "genes"), None), check_vma=False
    )
```

```python
import functools
import math

import jax
import jax.numpy as jnp
from jax import lax
from jax.experimental import pallas as pl
from jax.experimental.pallas import tpu as pltpu
from jax.sharding import PartitionSpec as P

ITERS = 2
epsilon = 1e-05
clip_top = 10.0
highest = lax.Precision.HIGHEST
f32 = jnp.float32
bf16 = jnp.bfloat16
LANES = 128
ROWS = 16
PIVOTS = 4
NT = (((1,), (1,)), ((), ()))


def split_two(value):
    high = value.astype(bf16)
    return high, (value - high.astype(f32)).astype(bf16)


def split_three(value):
    high = value.astype(bf16)
    rest = value - high.astype(f32)
    middle, low = split_two(rest)
    return high, middle, low


def inverse_factor(gram_folded):
    half_rows = gram_folded.shape[0]
    rank = 2 * half_rows
    lane = lax.broadcasted_iota(jnp.int32, (rank, 2 * rank), 1)
    row = lax.broadcasted_iota(jnp.int32, (rank, 2 * rank), 0)
    row_column = lax.broadcasted_iota(jnp.int32, (rank, 1), 0)
    gram = jnp.concatenate([gram_folded, pltpu.roll(gram_folded, rank, 1)], axis=0)
    both = jnp.where(lane < rank, gram, jnp.where(lane == row + rank, 1.0, 0.0))

    def step(turn, both):
        k = turn * PIVOTS
        rows = [
            jnp.sum(jnp.where(row == k + j, both, 0.0), axis=0, keepdims=True) for j in range(PIVOTS)
        ]
        columns = [
            jnp.sum(jnp.where(lane == k + j, both, 0.0), axis=1, keepdims=True)
            for j in range(PIVOTS)
        ]
        small = {}
        for j in range(PIVOTS):
            for m in range(j, PIVOTS):
                picked = jnp.where(row_column == k + j, columns[m], 0.0)
                small[j, m] = jnp.sum(picked, axis=0, keepdims=True)
        for j in range(PIVOTS):
            inverse = 1.0 / small[j, j]
            factor = jnp.where(row_column > k + j, columns[j] * inverse, 0.0)
            for m in range(j + 1, PIVOTS):
                ratio = small[j, m] * inverse
                columns[m] = columns[m] - factor * small[j, m]
                rows[m] = rows[m] - ratio * rows[j]
                for t in range(m, PIVOTS):
                    small[m, t] = small[m, t] - ratio * small[j, t]
            both = both - factor * rows[j]
        return both

    both = lax.fori_loop(0, rank // PIVOTS, step, both)
    diagonal = jnp.sum(jnp.where(lane == row, both, 0.0), axis=1, keepdims=True)
    return both[:, rank:] * lax.rsqrt(diagonal)


def kernel(
    cfg, counts_ref, basis_ref, out_ref,
    cnt, logs, xhi, xlo, tot, acc, center_ref, scale_ref, stat, wsplit,
    send_a, recv_a, send_b, recv_b, own_p, recv_p, product, gram_acc, inverse,
    shares, quarter_out, quarter_in, whole, gram_g, gram_c,
    load_sem, tot_sem, stat_sem, a_sem, b_send, b_recv, c_sem, rs_sem, x_sem, ag_sem, gg_sem, gc_sem,
):
    genes_dev, cells_dev, rank, groups, cell_devs, chunk, share_rows = cfg
    half_devs = cell_devs // 2
    set_cells = cells_dev * half_devs
    quarter = cells_dev // groups
    per_quarter = quarter // chunk
    steps = 2 * per_quarter
    gene = lax.axis_index("genes")
    cell = lax.axis_index("cells")
    y, core = gene // 2, gene % 2
    core_mate = {"genes": y * 2 + 1 - core}
    y_mate = {"genes": (1 - y) * 2 + core}
    dataset = cell // half_devs
    place = cell % half_devs
    cross = {"cells": (1 - dataset) * half_devs + place}

    def gene_peer(i):
        return {"genes": (gene + i) % groups}

    def set_place(i):
        return (place + i) % half_devs

    def set_peer(i):
        return {"cells": dataset * half_devs + set_place(i)}

    def remote(src, dst, send, recv, device):
        return pltpu.make_async_remote_copy(
            src_ref=src, dst_ref=dst, send_sem=send, recv_sem=recv,
            device_id=device, device_id_type=pl.DeviceIdType.MESH,
        )

    load_cols = cells_dev // 6 if cells_dev % (6 * LANES) == 0 else cells_dev
    loads = []
    for i in range(cells_dev // load_cols):
        cols = pl.ds(i * load_cols, load_cols)
        copy = pltpu.make_async_copy(counts_ref.at[:, cols], cnt.at[:, cols], load_sem.at[i])
        copy.start()
        loads.append(copy)

    barrier = pltpu.get_barrier_semaphore()
    mates = [gene_peer(i) for i in range(1, groups)]
    mates += [set_peer(i) for i in range(1, half_devs)] + [cross]
    for mate in mates:
        pl.semaphore_signal(barrier, inc=1, device_id=mate, device_id_type=pl.DeviceIdType.MESH)

    acc[...] = jnp.zeros_like(acc)
    stat[0] = jnp.zeros(stat.shape[1:], f32)
    for i, piece in enumerate(split_three(basis_ref[...])):
        wsplit[i * rank : (i + 1) * rank, :] = piece

    for i, copy in enumerate(loads):
        copy.wait()

        def add_genes(j, carry, base=i * load_cols):
            cols = pl.ds(pl.multiple_of(base + j * LANES, LANES), LANES)
            tot[0, :, cols] = jnp.sum(cnt[:, cols], axis=0, keepdims=True).astype(f32)
            return carry

        lax.fori_loop(0, load_cols // LANES, add_genes, 0)
    pl.semaphore_wait(barrier, len(mates))
    copies = [
        remote(tot.at[0], tot.at[i], tot_sem.at[0, i], tot_sem.at[1, i], gene_peer(i))
        for i in range(1, groups)
    ]
    for copy in copies:
        copy.start()
    for copy in copies:
        copy.wait()

    total = tot[0]
    for i in range(1, groups):
        total = total + tot[i]
    tot[0] = 10000.0 / total
    blocks = genes_dev // ROWS
    tail = blocks * ROWS
    logs[tail:, :] = jnp.zeros((logs.shape[0] - tail, cells_dev), f32)

    def over_rows(body):
        def block(r, carry):
            body(pl.ds(pl.multiple_of(r * ROWS, ROWS), ROWS))
            return carry

        lax.fori_loop(0, blocks, block, 0)
        if tail < genes_dev:
            body(pl.ds(tail, genes_dev - tail))

    def folded_sum(parts):
        while len(parts) > 1:
            parts = [sum(parts[i : i + 2]) for i in range(0, len(parts), 2)]
        return parts[0]

    starts = range(0, cells_dev, 4 * LANES)

    def to_logs(rows):
        running = None
        for start in starts:
            parts = []
            for low in range(start, start + 4 * LANES, LANES):
                cols = pl.ds(low, LANES)
                value = jnp.log(1.0 + cnt[rows, cols].astype(f32) * tot[0, :, cols])
                logs[rows, cols] = value
                parts.append(value)
            part = folded_sum(parts)
            running = part if running is None else running + part
        acc[rows, :] = running

    over_rows(to_logs)
    stat[0, 0:1, :] = jnp.sum(acc[...].T, axis=0, keepdims=True)
    center_ref[...] = jnp.broadcast_to(
        jnp.sum(acc[...], axis=1, keepdims=True) * (1.0 / cells_dev), center_ref.shape
    )

    def add_squares(rows):
        center = center_ref[rows, :]
        running = None
        for start in starts:
            parts = []
            for low in range(start, start + 4 * LANES, LANES):
                centered = logs[rows, pl.ds(low, LANES)] - center
                parts.append(centered * centered)
            part = folded_sum(parts)
            running = part if running is None else running + part
        acc[rows, :] = running

    over_rows(add_squares)
    stat[0, 1:2, :] = jnp.sum(acc[...].T, axis=0, keepdims=True)
    copies = [
        remote(stat.at[0], stat.at[i], stat_sem.at[0, i], stat_sem.at[1, i], set_peer(i))
        for i in range(1, half_devs)
    ]
    for copy in copies:
        copy.start()
    for copy in copies:
        copy.wait()
    gene_sum = stat[0, 0:1, :]
    for i in range(1, half_devs):
        gene_sum = gene_sum + stat[i, 0:1, :]
    center = gene_sum * (1.0 / set_cells)
    squares = jnp.zeros_like(center)
    for i in range(half_devs):
        shift = stat[i, 0:1, :] * (1.0 / cells_dev) - center
        squares = squares + (stat[i, 1:2, :] + cells_dev * (shift * shift))
    scale = 1.0 / jnp.sqrt(squares * (1.0 / set_cells) + epsilon)
    wide = (LANES, center.shape[1])
    center_ref[...] = jnp.broadcast_to(center, wide).T
    scale_ref[...] = jnp.broadcast_to(scale, wide).T

    def offset(k, half):
        return pl.multiple_of(
            (k // per_quarter) * (2 * quarter) + half * quarter + (k % per_quarter) * chunk, LANES
        )

    def scale_chunk(start):
        def block(r, carry):
            rows = pl.ds(pl.multiple_of(r * 2 * ROWS, 2 * ROWS), 2 * ROWS)
            center, scale = center_ref[rows, :], scale_ref[rows, :]
            for j in range(chunk // LANES):
                cols = pl.ds(pl.multiple_of(start + j * LANES, LANES), LANES)
                value = (logs[rows, cols] - center) * scale
                high, low = split_two(jnp.minimum(value, clip_top))
                xhi[rows, cols] = high
                xlo[rows, cols] = low
            return carry

        lax.fori_loop(0, xhi.shape[0] // (2 * ROWS), block, 0)

    def project(start):
        cols = pl.ds(start, chunk)
        top = jnp.dot(wsplit[...], xhi[:, cols], preferred_element_type=f32)
        rest = jnp.dot(wsplit[0 : 2 * rank, :], xlo[:, cols], preferred_element_type=f32)
        small = top[2 * rank :] + rest[rank:]
        return top[0:rank] + (top[rank : 2 * rank] + rest[0:rank] + small)

    def copy_a(k):
        return remote(send_a.at[k], recv_a.at[k], a_sem.at[0, k], a_sem.at[1, k], core_mate)

    def copy_c(k):
        return remote(own_p.at[k], recv_p.at[k], c_sem.at[0, k], c_sem.at[1, k], core_mate)

    def copy_b(stage, k, slot):
        return remote(
            send_b.at[k], recv_b.at[stage, slot], b_send.at[slot], b_recv.at[stage, slot], y_mate
        )

    def chip_sum(k, first):
        other = offset(k, 1 - core)
        if first:
            scale_chunk(other)
        send_a[k] = project(other)
        copy_a(k).start()
        mine = offset(k, core)
        if first:
            scale_chunk(mine)
        value = project(mine)
        copy_a(k).wait_recv()
        send_b[k] = value + recv_a[k]

    def add_gram(pieces):
        gram_acc[...] += lax.dot_general(pieces, pieces, NT, preferred_element_type=f32)

    def pieces_of(value):
        return jnp.concatenate(split_two(value), axis=0)

    def add_product(value, start):
        cols = pl.ds(start, chunk)
        pieces = pieces_of(value)
        product[...] += lax.dot_general(
            xhi[:, cols], pieces, NT, preferred_element_type=f32
        ) + lax.dot_general(xlo[:, cols], pieces, NT, preferred_element_type=f32)
        add_gram(pieces)

    lane_g = lax.broadcasted_iota(jnp.int32, (rank // 2, 2 * rank), 1)

    def folded_gram():
        gram = gram_acc[0:rank, :] + gram_acc[rank:, :]
        gram = gram + pltpu.roll(gram, rank, 1)
        return jnp.where(lane_g < rank, gram[0 : rank // 2], gram[rank // 2 :])

    fold = product.shape[0] // 2
    last = ITERS
    for stage in range(ITERS):
        product[...] = jnp.zeros_like(product)
        gram_acc[...] = jnp.zeros_like(gram_acc)

        def first_part(k, carry, stage=stage):
            chip_sum(k, stage == 0)
            copy_b(stage, k, k).start()
            return carry

        def second_part(k, carry, stage=stage):
            copy_b(stage, k, k).wait()
            value = send_b[k] + recv_b[stage, k]
            if stage > 0:
                value = jnp.dot(inverse[...], value, precision=highest, preferred_element_type=f32)
            own_p[k] = value
            copy_c(k).start()
            add_product(value, offset(k, core))
            copy_a(k).wait_send()
            copy_c(k).wait()
            add_product(recv_p[k], offset(k, 1 - core))
            return carry

        def both_parts(k, carry, stage=stage):
            first_part(k, carry)
            return second_part(k - lag, carry)

        lag = min(2, steps)
        lax.fori_loop(0, lag, first_part, 0)
        if stage > 0:
            inverse[...] = inverse_factor(whole[stage - 1, fold : fold + rank // 2, :])
        lax.fori_loop(lag, steps, both_parts, 0)
        lax.fori_loop(steps - lag, steps, second_part, 0)

        lane = lax.broadcasted_iota(jnp.int32, (fold, 2 * rank), 1)
        summed = product[...] + pltpu.roll(product[...], rank, 1)
        local = whole.at[ITERS + stage]
        local[0:fold, :] = jnp.where(lane < rank, summed[0:fold], summed[fold:])
        local[fold : fold + rank // 2, :] = folded_gram()
        if local.shape[0] > fold + rank // 2:
            rest = local.shape[0] - fold - rank // 2
            local[fold + rank // 2 :, :] = jnp.zeros((rest, 2 * rank), f32)

        def rows_of(index):
            return pl.ds(pl.multiple_of(index * share_rows, 8), share_rows)

        copies = [
            remote(
                local.at[rows_of(set_place(i))], shares.at[stage, i],
                rs_sem.at[0, stage, i], rs_sem.at[1, stage, i], set_peer(i),
            )
            for i in range(1, half_devs)
        ]
        for copy in copies:
            copy.start()
        for copy in copies:
            copy.wait()
        value = local[rows_of(place), :]
        for i in range(1, half_devs):
            value = value + shares[stage, i]
        quarter_out[stage] = value
        copy = remote(
            quarter_out.at[stage], quarter_in.at[stage], x_sem.at[0, stage], x_sem.at[1, stage], cross
        )
        copy.start()
        copy.wait()
        mine = rows_of(place)
        copies = [
            remote(
                quarter_in.at[stage], whole.at[stage, mine],
                ag_sem.at[0, stage, i], ag_sem.at[1, stage, i], set_peer(i),
            )
            for i in range(1, half_devs)
        ]
        for copy in copies:
            copy.start()
        whole[stage, mine, :] = quarter_in[stage]
        for copy in copies:
            copy.wait()
        turned = whole[stage, 0:fold, :].T
        for part, rows in ((0, turned[0:rank]), (1, turned[rank:])):
            for i, piece in enumerate(split_three(rows)):
                wsplit[i * rank : (i + 1) * rank, part * fold : (part + 1) * fold] = piece

    def send_loop(j, carry):
        k = (1 - y) * per_quarter + j
        chip_sum(k, False)
        copy_b(last, k, j).start()
        return carry

    lax.fori_loop(0, per_quarter, send_loop, 0)

    def keep_loop(j, carry):
        chip_sum(y * per_quarter + j, False)
        return carry

    lax.fori_loop(0, per_quarter, keep_loop, 0)
    gram_acc[...] = jnp.zeros_like(gram_acc)
    inverse[...] = inverse_factor(whole[ITERS - 1, fold : fold + rank // 2, :])

    def last_loop(j, carry):
        copy_b(last, y * per_quarter + j, j).wait()
        value = send_b[y * per_quarter + j] + recv_b[last, j]
        value = jnp.dot(inverse[...], value, precision=highest, preferred_element_type=f32)
        own_p[j] = value
        add_gram(pieces_of(value))
        copy_a(j).wait_send()
        copy_a(j + per_quarter).wait_send()
        return carry

    lax.fori_loop(0, per_quarter, last_loop, 0)
    gram_g[0] = folded_gram()
    copies = [
        remote(gram_g.at[0], gram_g.at[i], gg_sem.at[0, i], gg_sem.at[1, i], gene_peer(i))
        for i in range(1, groups)
    ]
    for copy in copies:
        copy.start()
    for copy in copies:
        copy.wait()
    value = gram_g[0]
    for i in range(1, groups):
        value = value + gram_g[i]
    gram_c[0] = value
    copies = [
        remote(gram_c.at[0], gram_c.at[i], gc_sem.at[0, i], gc_sem.at[1, i], set_peer(i))
        for i in range(1, half_devs)
    ]
    for copy in copies:
        copy.start()
    for copy in copies:
        copy.wait()
    for i in range(1, half_devs):
        value = value + gram_c[i]
    inverse[...] = inverse_factor(value) * math.sqrt(set_cells)
    for j in range(per_quarter):
        out_ref[:, j * chunk : (j + 1) * chunk] = jnp.dot(
            inverse[...], own_p[j], precision=highest, preferred_element_type=f32
        )


def shards(counts, start_basis):
    genes_dev, cells_dev = counts.shape
    rank = start_basis.shape[1]
    groups = lax.axis_size("genes")
    cell_devs = lax.axis_size("cells")
    assert groups == 4 and rank == 64
    half_devs = cell_devs // 2
    quarter = cells_dev // groups
    chunk = max(c for c in range(LANES, 512 + 1, LANES) if quarter % c == 0)
    steps = 2 * quarter // chunk
    padded = -(-genes_dev // 256) * 256
    rows = padded // 2 + rank // 2
    share_rows = -(-rows // (8 * half_devs)) * 8
    block = (rank, chunk)
    dma = pltpu.SemaphoreType.DMA
    scratch = [
        pltpu.VMEM((genes_dev, cells_dev), jnp.int32),
        pltpu.VMEM((padded, cells_dev), f32),
        pltpu.VMEM((padded, cells_dev), bf16),
        pltpu.VMEM((padded, cells_dev), bf16),
        pltpu.VMEM((groups, 1, cells_dev), f32),
        pltpu.VMEM((padded, LANES), f32),
        pltpu.VMEM((padded, LANES), f32),
        pltpu.VMEM((padded, LANES), f32),
        pltpu.VMEM((half_devs, 8, padded), f32),
        pltpu.VMEM((3 * rank, padded), bf16),
        pltpu.VMEM((steps,) + block, f32),
        pltpu.VMEM((steps,) + block, f32),
        pltpu.VMEM((steps,) + block, f32),
        pltpu.VMEM((ITERS + 1, steps) + block, f32),
        pltpu.VMEM((steps,) + block, f32),
        pltpu.VMEM((steps,) + block, f32),
        pltpu.VMEM((padded, 2 * rank), f32),
        pltpu.VMEM((2 * rank, 2 * rank), f32),
        pltpu.VMEM((rank, rank), f32),
        pltpu.VMEM((ITERS, half_devs, share_rows, 2 * rank), f32),
        pltpu.VMEM((ITERS, share_rows, 2 * rank), f32),
        pltpu.VMEM((ITERS, share_rows, 2 * rank), f32),
        pltpu.VMEM((2 * ITERS, share_rows * half_devs, 2 * rank), f32),
        pltpu.VMEM((groups, rank // 2, 2 * rank), f32),
        pltpu.VMEM((half_devs, rank // 2, 2 * rank), f32),
        dma((6,)),
        dma((2, groups)),
        dma((2, half_devs)),
        dma((2, steps)),
        dma((steps,)),
        dma((ITERS + 1, steps)),
        dma((2, steps)),
        dma((2, ITERS, half_devs)),
        dma((2, ITERS)),
        dma((2, ITERS, half_devs)),
        dma((2, groups)),
        dma((2, half_devs)),
    ]
    cfg = (genes_dev, cells_dev, rank, groups, cell_devs, chunk, share_rows)
    flops = 2 * 5 * 4 * genes_dev * cells_dev * rank
    turned = pl.pallas_call(
        functools.partial(kernel, cfg),
        out_shape=jax.ShapeDtypeStruct((rank, quarter), f32),
        in_specs=[pl.BlockSpec(memory_space=pl.ANY), pl.BlockSpec(memory_space=pltpu.VMEM)],
        out_specs=pl.BlockSpec(memory_space=pltpu.VMEM),
        scratch_shapes=scratch,
        compiler_params=pltpu.CompilerParams(
            collective_id=0, has_side_effects=True, vmem_limit_bytes=60 * 2**20
        ),
        cost_estimate=pl.CostEstimate(
            flops=flops, bytes_accessed=4 * genes_dev * cells_dev,
            transcendentals=genes_dev * cells_dev,
        ),
    )(counts, jnp.pad(start_basis, ((0, padded - genes_dev), (0, 0))).T)
    return turned.T


def solution(mesh):
    placed = (P("genes", "cells"), P("genes", None))
    return jax.shard_map(
        shards, mesh=mesh, in_specs=placed, out_specs=P(("cells", "genes"), None), check_vma=False
    )
```

```python
import functools
import math

import jax
import jax.numpy as jnp
from jax import lax
from jax.experimental import pallas as pl
from jax.experimental.pallas import tpu as pltpu
from jax.sharding import PartitionSpec as P

ITERS = 2
epsilon = 1e-05
clip_top = 10.0
highest = lax.Precision.HIGHEST
f32 = jnp.float32
bf16 = jnp.bfloat16
LANES = 128
ROWS = 16
PIVOTS = 4
NT = (((1,), (1,)), ((), ()))


def split_two(value):
    high = value.astype(bf16)
    return high, (value - high.astype(f32)).astype(bf16)


def split_three(value):
    high = value.astype(bf16)
    rest = value - high.astype(f32)
    middle, low = split_two(rest)
    return high, middle, low


def elimination_grids(rank):
    lane = lax.broadcasted_iota(jnp.int32, (rank, 2 * rank), 1)
    row = lax.broadcasted_iota(jnp.int32, (rank, 2 * rank), 0)
    return lane, row


def elimination_start(gram_folded):
    rank = 2 * gram_folded.shape[0]
    lane, row = elimination_grids(rank)
    gram = jnp.concatenate([gram_folded, pltpu.roll(gram_folded, rank, 1)], axis=0)
    return jnp.where(lane < rank, gram, jnp.where(lane == row + rank, 1.0, 0.0))


def elimination_run(both, first, stop):
    rank = both.shape[0]
    lane, row = elimination_grids(rank)
    row_column = lax.broadcasted_iota(jnp.int32, (rank, 1), 0)

    def step(turn, both):
        k = turn * PIVOTS
        rows = [
            jnp.sum(jnp.where(row == k + j, both, 0.0), axis=0, keepdims=True) for j in range(PIVOTS)
        ]
        columns = [
            jnp.sum(jnp.where(lane == k + j, both, 0.0), axis=1, keepdims=True)
            for j in range(PIVOTS)
        ]
        small = {}
        for j in range(PIVOTS):
            for m in range(j, PIVOTS):
                picked = jnp.where(row_column == k + j, columns[m], 0.0)
                small[j, m] = jnp.sum(picked, axis=0, keepdims=True)
        for j in range(PIVOTS):
            inverse = 1.0 / small[j, j]
            factor = jnp.where(row_column > k + j, columns[j] * inverse, 0.0)
            for m in range(j + 1, PIVOTS):
                ratio = small[j, m] * inverse
                columns[m] = columns[m] - factor * small[j, m]
                rows[m] = rows[m] - ratio * rows[j]
                for t in range(m, PIVOTS):
                    small[m, t] = small[m, t] - ratio * small[j, t]
            both = both - factor * rows[j]
        return both

    return lax.fori_loop(first, stop, step, both)


def elimination_end(both):
    rank = both.shape[0]
    lane, row = elimination_grids(rank)
    diagonal = jnp.sum(jnp.where(lane == row, both, 0.0), axis=1, keepdims=True)
    return both[:, rank:] * lax.rsqrt(diagonal)


def inverse_factor(gram_folded):
    both = elimination_start(gram_folded)
    return elimination_end(elimination_run(both, 0, both.shape[0] // PIVOTS))


def kernel(
    cfg, counts_ref, basis_ref, out_ref,
    cnt, logs, xhi, xlo, tot, acc, center_ref, scale_ref, stat, wsplit,
    send_a, recv_a, send_b, recv_b, own_p, recv_p, product, gram_acc, inverse,
    shares, quarter_out, quarter_in, whole, gram_in, gram_g, gram_c,
    load_sem, tot_sem, stat_sem, a_sem, b_send, b_recv, c_sem, rs_sem, x_sem, ag_sem, gs_sem, gg_sem, gc_sem,
):
    genes_dev, cells_dev, rank, groups, cell_devs, chunk, share_rows = cfg
    half_devs = cell_devs // 2
    set_cells = cells_dev * half_devs
    quarter = cells_dev // groups
    per_quarter = quarter // chunk
    steps = 2 * per_quarter
    gene = lax.axis_index("genes")
    cell = lax.axis_index("cells")
    y, core = gene // 2, gene % 2
    core_mate = {"genes": y * 2 + 1 - core}
    y_mate = {"genes": (1 - y) * 2 + core}
    dataset = cell // half_devs
    place = cell % half_devs

    def gene_peer(i):
        return {"genes": (gene + i) % groups}

    def set_place(i):
        return (place + i) % half_devs

    def set_peer(i):
        return {"cells": dataset * half_devs + set_place(i)}

    def cross_peer(i):
        return {"cells": (1 - dataset) * half_devs + set_place(i)}

    def remote(src, dst, send, recv, device):
        return pltpu.make_async_remote_copy(
            src_ref=src, dst_ref=dst, send_sem=send, recv_sem=recv,
            device_id=device, device_id_type=pl.DeviceIdType.MESH,
        )

    load_cols = cells_dev // 6 if cells_dev % (6 * LANES) == 0 else cells_dev
    loads = []
    for i in range(cells_dev // load_cols):
        cols = pl.ds(i * load_cols, load_cols)
        copy = pltpu.make_async_copy(counts_ref.at[:, cols], cnt.at[:, cols], load_sem.at[i])
        copy.start()
        loads.append(copy)

    barrier = pltpu.get_barrier_semaphore()
    mates = [gene_peer(i) for i in range(1, groups)]
    mates += [set_peer(i) for i in range(1, half_devs)]
    mates += [cross_peer(i) for i in range(half_devs)]
    for mate in mates:
        pl.semaphore_signal(barrier, inc=1, device_id=mate, device_id_type=pl.DeviceIdType.MESH)

    acc[...] = jnp.zeros_like(acc)
    stat[0] = jnp.zeros(stat.shape[1:], f32)
    for i, piece in enumerate(split_three(basis_ref[...])):
        wsplit[i * rank : (i + 1) * rank, :] = piece

    for i, copy in enumerate(loads):
        copy.wait()

        def add_genes(j, carry, base=i * load_cols):
            cols = pl.ds(pl.multiple_of(base + j * LANES, LANES), LANES)
            tot[0, :, cols] = jnp.sum(cnt[:, cols], axis=0, keepdims=True).astype(f32)
            return carry

        lax.fori_loop(0, load_cols // LANES, add_genes, 0)
    pl.semaphore_wait(barrier, len(mates))
    copies = [
        remote(tot.at[0], tot.at[i], tot_sem.at[0, i], tot_sem.at[1, i], gene_peer(i))
        for i in range(1, groups)
    ]
    for copy in copies:
        copy.start()
    for copy in copies:
        copy.wait()

    total = tot[0]
    for i in range(1, groups):
        total = total + tot[i]
    tot[0] = 10000.0 / total
    blocks = genes_dev // ROWS
    tail = blocks * ROWS
    logs[tail:, :] = jnp.zeros((logs.shape[0] - tail, cells_dev), f32)

    def over_rows(body):
        def block(r, carry):
            body(pl.ds(pl.multiple_of(r * ROWS, ROWS), ROWS))
            return carry

        lax.fori_loop(0, blocks, block, 0)
        if tail < genes_dev:
            body(pl.ds(tail, genes_dev - tail))

    def folded_sum(parts):
        while len(parts) > 1:
            parts = [sum(parts[i : i + 2]) for i in range(0, len(parts), 2)]
        return parts[0]

    starts = range(0, cells_dev, 4 * LANES)

    def to_logs(rows):
        running = None
        for start in starts:
            parts = []
            for low in range(start, start + 4 * LANES, LANES):
                cols = pl.ds(low, LANES)
                value = jnp.log(1.0 + cnt[rows, cols].astype(f32) * tot[0, :, cols])
                logs[rows, cols] = value
                parts.append(value)
            part = folded_sum(parts)
            running = part if running is None else running + part
        acc[rows, :] = running

    over_rows(to_logs)
    stat[0, 0:1, :] = jnp.sum(acc[...].T, axis=0, keepdims=True)
    center_ref[...] = jnp.broadcast_to(
        jnp.sum(acc[...], axis=1, keepdims=True) * (1.0 / cells_dev), center_ref.shape
    )

    def add_squares(rows):
        center = center_ref[rows, :]
        running = None
        for start in starts:
            parts = []
            for low in range(start, start + 4 * LANES, LANES):
                centered = logs[rows, pl.ds(low, LANES)] - center
                parts.append(centered * centered)
            part = folded_sum(parts)
            running = part if running is None else running + part
        acc[rows, :] = running

    over_rows(add_squares)
    stat[0, 1:2, :] = jnp.sum(acc[...].T, axis=0, keepdims=True)
    copies = [
        remote(stat.at[0], stat.at[i], stat_sem.at[0, i], stat_sem.at[1, i], set_peer(i))
        for i in range(1, half_devs)
    ]
    for copy in copies:
        copy.start()
    for copy in copies:
        copy.wait()
    gene_sum = stat[0, 0:1, :]
    for i in range(1, half_devs):
        gene_sum = gene_sum + stat[i, 0:1, :]
    center = gene_sum * (1.0 / set_cells)
    squares = jnp.zeros_like(center)
    for i in range(half_devs):
        shift = stat[i, 0:1, :] * (1.0 / cells_dev) - center
        squares = squares + (stat[i, 1:2, :] + cells_dev * (shift * shift))
    scale = 1.0 / jnp.sqrt(squares * (1.0 / set_cells) + epsilon)
    wide = (LANES, center.shape[1])
    center_ref[...] = jnp.broadcast_to(center, wide).T
    scale_ref[...] = jnp.broadcast_to(scale, wide).T

    def offset(k, half):
        return pl.multiple_of(
            (k // per_quarter) * (2 * quarter) + half * quarter + (k % per_quarter) * chunk, LANES
        )

    def scale_chunk(start):
        def block(r, carry):
            rows = pl.ds(pl.multiple_of(r * 2 * ROWS, 2 * ROWS), 2 * ROWS)
            center, scale = center_ref[rows, :], scale_ref[rows, :]
            for j in range(chunk // LANES):
                cols = pl.ds(pl.multiple_of(start + j * LANES, LANES), LANES)
                value = (logs[rows, cols] - center) * scale
                high, low = split_two(jnp.minimum(value, clip_top))
                xhi[rows, cols] = high
                xlo[rows, cols] = low
            return carry

        lax.fori_loop(0, xhi.shape[0] // (2 * ROWS), block, 0)

    def project(start):
        cols = pl.ds(start, chunk)
        top = jnp.dot(wsplit[...], xhi[:, cols], preferred_element_type=f32)
        rest = jnp.dot(wsplit[0 : 2 * rank, :], xlo[:, cols], preferred_element_type=f32)
        small = top[2 * rank :] + rest[rank:]
        return top[0:rank] + (top[rank : 2 * rank] + rest[0:rank] + small)

    def copy_a(k):
        return remote(send_a.at[k], recv_a.at[k], a_sem.at[0, k], a_sem.at[1, k], core_mate)

    def copy_c(k):
        return remote(own_p.at[k], recv_p.at[k], c_sem.at[0, k], c_sem.at[1, k], core_mate)

    def copy_b(stage, k, slot):
        return remote(
            send_b.at[k], recv_b.at[stage, slot], b_send.at[slot], b_recv.at[stage, slot], y_mate
        )

    def chip_sum(k, first):
        other = offset(k, 1 - core)
        if first:
            scale_chunk(other)
        send_a[k] = project(other)
        copy_a(k).start()
        mine = offset(k, core)
        if first:
            scale_chunk(mine)
        value = project(mine)
        copy_a(k).wait_recv()
        send_b[k] = value + recv_a[k]

    def add_gram(pieces):
        gram_acc[...] += lax.dot_general(pieces, pieces, NT, preferred_element_type=f32)

    def pieces_of(value):
        return jnp.concatenate(split_two(value), axis=0)

    def add_product(value, start):
        cols = pl.ds(start, chunk)
        pieces = pieces_of(value)
        product[...] += lax.dot_general(
            xhi[:, cols], pieces, NT, preferred_element_type=f32
        ) + lax.dot_general(xlo[:, cols], pieces, NT, preferred_element_type=f32)
        add_gram(pieces)

    lane_g = lax.broadcasted_iota(jnp.int32, (rank // 2, 2 * rank), 1)

    def folded_gram():
        gram = gram_acc[0:rank, :] + gram_acc[rank:, :]
        gram = gram + pltpu.roll(gram, rank, 1)
        return jnp.where(lane_g < rank, gram[0 : rank // 2], gram[rank // 2 :])

    fold = product.shape[0] // 2
    last = ITERS
    for stage in range(ITERS):
        product[...] = jnp.zeros_like(product)
        gram_acc[...] = jnp.zeros_like(gram_acc)

        def first_part(k, carry, stage=stage):
            chip_sum(k, stage == 0)
            copy_b(stage, k, k).start()
            return carry

        def second_part(k, carry, stage=stage):
            copy_b(stage, k, k).wait()
            value = send_b[k] + recv_b[stage, k]
            if stage > 0:
                value = jnp.dot(inverse[...], value, precision=highest, preferred_element_type=f32)
            own_p[k] = value
            copy_c(k).start()
            add_product(value, offset(k, core))
            copy_a(k).wait_send()
            copy_c(k).wait()
            add_product(recv_p[k], offset(k, 1 - core))
            return carry

        def both_parts(k, carry, stage=stage):
            first_part(k, carry)
            return second_part(k - lag, carry)

        lag = min(2, steps)
        lax.fori_loop(0, lag, first_part, 0)
        lax.fori_loop(lag, steps, both_parts, 0)
        lax.fori_loop(steps - lag, steps, second_part, 0)

        gram_acc[0 : rank // 2, :] = folded_gram()
        gram_copies = [
            remote(
                gram_acc.at[0 : rank // 2], gram_in.at[stage, place],
                gs_sem.at[0, stage, i], gs_sem.at[1, stage, i], cross_peer(i),
            )
            for i in range(half_devs)
        ]
        for copy in gram_copies:
            copy.start()
        lane = lax.broadcasted_iota(jnp.int32, (fold, 2 * rank), 1)
        summed = product[...] + pltpu.roll(product[...], rank, 1)
        local = whole.at[ITERS + stage]
        local[0:fold, :] = jnp.where(lane < rank, summed[0:fold], summed[fold:])
        if local.shape[0] > fold:
            local[fold:, :] = jnp.zeros((local.shape[0] - fold, 2 * rank), f32)

        def rows_of(index):
            return pl.ds(pl.multiple_of(index * share_rows, 8), share_rows)

        copies = [
            remote(
                local.at[rows_of(set_place(i))], shares.at[stage, i],
                rs_sem.at[0, stage, i], rs_sem.at[1, stage, i], set_peer(i),
            )
            for i in range(1, half_devs)
        ]
        for copy in copies:
            copy.start()
        for copy in copies:
            copy.wait()
        value = local[rows_of(place), :]
        for i in range(1, half_devs):
            value = value + shares[stage, i]
        quarter_out[stage] = value
        copy = remote(
            quarter_out.at[stage], quarter_in.at[stage], x_sem.at[0, stage], x_sem.at[1, stage], cross_peer(0)
        )
        copy.start()
        for gram_copy in gram_copies:
            gram_copy.wait()
        value = gram_in[stage, 0]
        for i in range(1, half_devs):
            value = value + gram_in[stage, i]
        turns = rank // PIVOTS
        both = elimination_run(elimination_start(value), 0, turns // 2)
        copy.wait()
        mine = rows_of(place)
        copies = [
            remote(
                quarter_in.at[stage], whole.at[stage, mine],
                ag_sem.at[0, stage, i], ag_sem.at[1, stage, i], set_peer(i),
            )
            for i in range(1, half_devs)
        ]
        for copy in copies:
            copy.start()
        whole[stage, mine, :] = quarter_in[stage]
        inverse[...] = elimination_end(elimination_run(both, turns // 2, turns))
        for copy in copies:
            copy.wait()
        turned = whole[stage, 0:fold, :].T
        for part, rows in ((0, turned[0:rank]), (1, turned[rank:])):
            for i, piece in enumerate(split_three(rows)):
                wsplit[i * rank : (i + 1) * rank, part * fold : (part + 1) * fold] = piece

    def send_loop(j, carry):
        k = (1 - y) * per_quarter + j
        chip_sum(k, False)
        copy_b(last, k, j).start()
        return carry

    lax.fori_loop(0, per_quarter, send_loop, 0)

    def keep_loop(j, carry):
        chip_sum(y * per_quarter + j, False)
        return carry

    lax.fori_loop(0, per_quarter, keep_loop, 0)
    gram_acc[...] = jnp.zeros_like(gram_acc)

    def last_loop(j, carry):
        copy_b(last, y * per_quarter + j, j).wait()
        value = send_b[y * per_quarter + j] + recv_b[last, j]
        value = jnp.dot(inverse[...], value, precision=highest, preferred_element_type=f32)
        own_p[j] = value
        add_gram(pieces_of(value))
        copy_a(j).wait_send()
        copy_a(j + per_quarter).wait_send()
        return carry

    lax.fori_loop(0, per_quarter, last_loop, 0)
    gram_g[0] = folded_gram()
    copies = [
        remote(gram_g.at[0], gram_g.at[i], gg_sem.at[0, i], gg_sem.at[1, i], gene_peer(i))
        for i in range(1, groups)
    ]
    for copy in copies:
        copy.start()
    for copy in copies:
        copy.wait()
    value = gram_g[0]
    for i in range(1, groups):
        value = value + gram_g[i]
    gram_c[0] = value
    copies = [
        remote(gram_c.at[0], gram_c.at[i], gc_sem.at[0, i], gc_sem.at[1, i], set_peer(i))
        for i in range(1, half_devs)
    ]
    for copy in copies:
        copy.start()
    for copy in copies:
        copy.wait()
    for i in range(1, half_devs):
        value = value + gram_c[i]
    inverse[...] = inverse_factor(value) * math.sqrt(set_cells)
    for j in range(per_quarter):
        out_ref[:, j * chunk : (j + 1) * chunk] = jnp.dot(
            inverse[...], own_p[j], precision=highest, preferred_element_type=f32
        )


def shards(counts, start_basis):
    genes_dev, cells_dev = counts.shape
    rank = start_basis.shape[1]
    groups = lax.axis_size("genes")
    cell_devs = lax.axis_size("cells")
    assert groups == 4 and rank == 64
    half_devs = cell_devs // 2
    quarter = cells_dev // groups
    chunk = max(c for c in range(LANES, 512 + 1, LANES) if quarter % c == 0)
    steps = 2 * quarter // chunk
    padded = -(-genes_dev // 256) * 256
    share_rows = -(-padded // 2 // (8 * half_devs)) * 8
    block = (rank, chunk)
    dma = pltpu.SemaphoreType.DMA
    scratch = [
        pltpu.VMEM((genes_dev, cells_dev), jnp.int32),
        pltpu.VMEM((padded, cells_dev), f32),
        pltpu.VMEM((padded, cells_dev), bf16),
        pltpu.VMEM((padded, cells_dev), bf16),
        pltpu.VMEM((groups, 1, cells_dev), f32),
        pltpu.VMEM((padded, LANES), f32),
        pltpu.VMEM((padded, LANES), f32),
        pltpu.VMEM((padded, LANES), f32),
        pltpu.VMEM((half_devs, 8, padded), f32),
        pltpu.VMEM((3 * rank, padded), bf16),
        pltpu.VMEM((steps,) + block, f32),
        pltpu.VMEM((steps,) + block, f32),
        pltpu.VMEM((steps,) + block, f32),
        pltpu.VMEM((ITERS + 1, steps) + block, f32),
        pltpu.VMEM((steps,) + block, f32),
        pltpu.VMEM((steps,) + block, f32),
        pltpu.VMEM((padded, 2 * rank), f32),
        pltpu.VMEM((2 * rank, 2 * rank), f32),
        pltpu.VMEM((rank, rank), f32),
        pltpu.VMEM((ITERS, half_devs, share_rows, 2 * rank), f32),
        pltpu.VMEM((ITERS, share_rows, 2 * rank), f32),
        pltpu.VMEM((ITERS, share_rows, 2 * rank), f32),
        pltpu.VMEM((2 * ITERS, share_rows * half_devs, 2 * rank), f32),
        pltpu.VMEM((ITERS, half_devs, rank // 2, 2 * rank), f32),
        pltpu.VMEM((groups, rank // 2, 2 * rank), f32),
        pltpu.VMEM((half_devs, rank // 2, 2 * rank), f32),
        dma((6,)),
        dma((2, groups)),
        dma((2, half_devs)),
        dma((2, steps)),
        dma((steps,)),
        dma((ITERS + 1, steps)),
        dma((2, steps)),
        dma((2, ITERS, half_devs)),
        dma((2, ITERS)),
        dma((2, ITERS, half_devs)),
        dma((2, ITERS, half_devs)),
        dma((2, groups)),
        dma((2, half_devs)),
    ]
    cfg = (genes_dev, cells_dev, rank, groups, cell_devs, chunk, share_rows)
    flops = 2 * 5 * 4 * genes_dev * cells_dev * rank
    turned = pl.pallas_call(
        functools.partial(kernel, cfg),
        out_shape=jax.ShapeDtypeStruct((rank, quarter), f32),
        in_specs=[pl.BlockSpec(memory_space=pl.ANY), pl.BlockSpec(memory_space=pltpu.VMEM)],
        out_specs=pl.BlockSpec(memory_space=pltpu.VMEM),
        scratch_shapes=scratch,
        compiler_params=pltpu.CompilerParams(
            collective_id=0, has_side_effects=True, vmem_limit_bytes=60 * 2**20
        ),
        cost_estimate=pl.CostEstimate(
            flops=flops, bytes_accessed=4 * genes_dev * cells_dev,
            transcendentals=genes_dev * cells_dev,
        ),
    )(counts, jnp.pad(start_basis, ((0, padded - genes_dev), (0, 0))).T)
    return turned.T


def solution(mesh):
    placed = (P("genes", "cells"), P("genes", None))
    return jax.shard_map(
        shards, mesh=mesh, in_specs=placed, out_specs=P(("cells", "genes"), None), check_vma=False
    )
```
